32 devices in a mesh: groups: 2 (over y), dp: 4 (over x, core), layer: 4 (over z).
Axes of the slice: x: 2, y: 2, z: 4, core: 2. Of those that a mesh axis runs over, the one named last changes fastest.
Arguments:
- train_grads: bfloat16 [8192, 4, 4096], P(('groups', 'dp'), 'layer'), parts along dimension 0, may hold values from -6 to 6
- query_grads: bfloat16 [512, 4, 4096], P('dp', 'layer'), may hold values from -6 to 6
- basis_out: float32 [4, 64, 64], P('layer'), may hold values from -0.75 to 0.75
- basis_in: float32 [4, 64, 64], P('layer'), may hold values from -0.75 to 0.75
- scaling: float32 [4, 64, 64], P('layer'), may hold values from 0.05 to 2
Outputs:
- scores: float32 [512, 8192], P('layer', ('groups', 'dp')), parts along dimension 1
The draws below stay inside these ranges and needn't reach their ends.
There are 2 independent parts, one for each index of `groups`. The reference program is written for one: setup_inputs(seed, part) draws one part's arguments, and reference() takes and returns one part's arrays. A program takes and returns all parts, laid end to end along the dimension named above; an argument that names none is the same for every part. Nothing has to cross between parts.
All inputs are finite; a program needn't handle non-finite values.
Results may differ from the reference program's by a relative error of at most 0.0029.
Values may be sent and summed in bfloat16 or wider, within the bound.
A program may use at most 192 MiB of HBM per device.

```python
import math
import jax
import jax.numpy as jnp
from jax import lax

PIN = 64
POUT = 64
K = 4096
LAYERS = 4
NTRAIN = 4096
QUERIES = 512


def block_levels(own_key, extent, pieces, least, top_value):
    loudness = 1.0
    for position, shards_of in pieces:
        steps = jax.random.uniform(jax.random.fold_in(jax.random.fold_in(own_key, 6), position), (shards_of,), jnp.float32, least / len(pieces), top_value / len(pieces))
        loudness = loudness * jnp.repeat(jnp.exp(steps), extent[position] // shards_of).reshape((-1,) + (1,) * (len(extent) - 1 - position))
    return loudness


def normal_values(own_key, shape, width, reach, cuts=(), kind=jnp.bfloat16):
    factor_of = block_levels(own_key, shape, cuts, -0.22, 0.18) if cuts else 1.0
    drawn = jax.random.normal(own_key, shape, jnp.float32) * width * factor_of
    return jnp.minimum(jnp.maximum(drawn, -reach), reach).astype(kind)


def setup_inputs(seed: int = 0, part: int = 0) -> dict:
    key_list = jax.random.split(jax.random.key(seed), 6)
    part_keys = jax.random.split(jax.random.fold_in(key_list[5], part), 6)
    train_grads = normal_values(part_keys[0], (NTRAIN, LAYERS, K), 1.0, 6.0, ((0, 4), (1, 4)))
    query_grads = normal_values(key_list[1], (QUERIES, LAYERS, K), 1.0, 6.0, ((0, 4), (1, 4)))
    basis_out = normal_values(key_list[2], (LAYERS, POUT, POUT), POUT ** -0.5, 0.75, ((0, 4),), jnp.float32)
    basis_in = normal_values(key_list[3], (LAYERS, PIN, PIN), PIN ** -0.5, 0.75, ((0, 4),), jnp.float32)
    scaling = jnp.clip(jnp.exp(math.log(2.0) - 3.6888794 * jax.random.uniform(key_list[4], (LAYERS, POUT, PIN), jnp.float32) ** block_levels(key_list[4], (LAYERS, POUT, PIN), ((0, 4),), -0.2, 0.2)), 0.05, 2.0)
    return {"train_grads": train_grads, "query_grads": query_grads, "basis_out": basis_out, "basis_in": basis_in, "scaling": scaling}


damping = 0.1


def precondition(grads, out_basis, in_basis, corrected):
    count = grads.shape[0]
    matrix = grads.astype(jnp.float32).reshape(count, out_basis.shape[0], in_basis.shape[0])
    hp = lax.Precision.HIGHEST
    right = jnp.einsum('mcb,bd->mcd', matrix, in_basis, precision=hp)
    rotated = jnp.einsum('ca,mcd->mad', out_basis, right, precision=hp)
    damped = rotated / (corrected + damping)
    back = jnp.einsum('mad,ed->mae', damped, in_basis, precision=hp)
    result = jnp.einsum('ca,mae->mce', out_basis, back, precision=hp)
    return result.reshape(count, -1).astype(jnp.bfloat16)


def reference(train_grads, query_grads, basis_out, basis_in, scaling):
    total = jnp.zeros((query_grads.shape[0], train_grads.shape[0]), jnp.float32)
    for layer_index in range(LAYERS):
        ready = precondition(query_grads[:, layer_index, :], basis_out[layer_index], basis_in[layer_index], scaling[layer_index])
        total = total + jnp.einsum('mk,nk->mn', ready, train_grads[:, layer_index, :], preferred_element_type=jnp.float32)
    return total
```

```python
import functools

import jax
import jax.numpy as jnp
from jax import lax
from jax.experimental import pallas as pl
from jax.experimental.pallas import tpu as pltpu
from jax.sharding import PartitionSpec as P

damping = 0.1
f32 = jnp.float32
bf16 = jnp.bfloat16
MESH = pl.DeviceIdType.MESH
VMEM_LIMIT = 56 * 1024 * 1024
NT = (((1,), (1,)), ((), ()))
D = 64
CHUNK = 16


def dot_nt(a, b):
    return lax.dot_general(a, b, NT, preferred_element_type=f32)


def high_low(x):
    high = x.astype(bf16)
    return high, (x - high.astype(f32)).astype(bf16)


def lane_split(x):
    high, low = high_low(x)
    lane = lax.broadcasted_iota(jnp.int32, x.shape, 1)
    return jnp.where((lane // D) % 2 == 0, high.astype(f32), low.astype(f32)).astype(bf16)


def row_split(x):
    high, low = high_low(x)
    return jnp.concatenate([high, high, low, low], axis=0)


def precondition_kernel(
    g_ref, bo_ref, bi_ref, s_ref, p_ref, wide, tall, square, rot, back, bo4, bi4, d4, w_in
):
    count = g_ref.shape[0]
    bo, bi = bo_ref[...], bi_ref[...]
    inverse = 1.0 / (s_ref[...] + damping)

    for j in range(4):
        bo4[:, j * D : (j + 1) * D] = bo
        bi4[:, j * D : (j + 1) * D] = bi
        for i in range(4):
            wide[i * D : (i + 1) * D, j * D : (j + 1) * D] = bo
    lane = lax.broadcasted_iota(jnp.int32, wide.shape, 1)
    high, low = high_low(wide[...])
    wide_split = jnp.where(lane < 2 * D, high.astype(f32), low.astype(f32)).astype(bf16)
    tall[...] = jnp.zeros_like(tall)
    for j in range(4):
        tall[j * D : (j + 1) * D, 0:D] = inverse
    d4[...] = jnp.transpose(tall[...])
    square[...] = jnp.zeros_like(square)
    square[0:D, 0:D] = bi
    square[D : 2 * D, D : 2 * D] = bi
    high, low = high_low(jnp.transpose(square[...]))
    w_in[...] = jnp.concatenate([high, low], axis=1)
    bi4_split = lane_split(bi4[...])

    weights = w_in[...]
    for pair in range(D // 2):
        block = g_ref[:, pair * 2 * D : (pair + 1) * 2 * D]
        rot[pair * 2 * D : (pair + 1) * 2 * D, :] = dot_nt(
            weights, jnp.concatenate([block, block], axis=1)
        )

    bo_four = bo4[...]
    group = 8

    def middle(step, carry):
        first = step * group
        scales = d4[pl.ds(pl.multiple_of(first, group), group), :]
        left = jnp.concatenate(
            [lane_split(bo_four * scales[i : i + 1, :]) for i in range(group)], axis=0
        )
        mats = lane_split(dot_nt(left, wide_split))
        for i in range(group):
            column = rot[pl.ds(first + i, D, stride=D), :]
            back[pl.ds(pl.multiple_of((first + i) * D, D), D), :] = jnp.dot(
                mats[i * D : (i + 1) * D, :], row_split(column), preferred_element_type=f32
            )
        return carry

    lax.fori_loop(0, D // group, middle, 0)

    for pair in range(D // 2):
        halves = [
            jnp.dot(
                bi4_split,
                row_split(back[pl.ds(2 * pair + i, D, stride=D), :]),
                preferred_element_type=f32,
            )
            for i in range(2)
        ]
        block = jnp.transpose(jnp.concatenate(halves, axis=0))
        p_ref[:, pair * 2 * D : (pair + 1) * 2 * D] = block.astype(bf16)


def precondition(grads, bo, bi, s):
    count, entries = grads.shape
    vmem = pl.BlockSpec(memory_space=pltpu.VMEM)
    return pl.pallas_call(
        precondition_kernel,
        out_shape=jax.ShapeDtypeStruct((count, entries), bf16),
        in_specs=[vmem] * 4,
        out_specs=vmem,
        scratch_shapes=[
            pltpu.VMEM((4 * D, 4 * D), f32),
            pltpu.VMEM((4 * D, 2 * D), f32),
            pltpu.VMEM((2 * D, 2 * D), f32),
            pltpu.VMEM((entries, count), f32),
            pltpu.VMEM((entries, count), f32),
            pltpu.VMEM((D, 4 * D), f32),
            pltpu.VMEM((D, 4 * D), f32),
            pltpu.VMEM((2 * D, 4 * D), f32),
            pltpu.VMEM((2 * D, 4 * D), bf16),
        ],
        compiler_params=pltpu.CompilerParams(vmem_limit_bytes=VMEM_LIMIT),
        name="precondition",
    )(grads, bo, bi, s)


def score_kernel(
    sizes,
    train_hbm,
    p_ref,
    out_ref,
    train,
    every,
    ours,
    theirs,
    train_sem,
    far_send,
    far_recv,
    row_send,
    row_recv,
    core_send,
    core_recv,
    sum_send,
    sum_recv,
):
    dp, layers = sizes
    chips = dp // 2
    per = dp // layers
    half = p_ref.shape[0] // 2
    chunks = half // CHUNK
    n = train.shape[0]
    y = lax.axis_index("groups")
    me = lax.axis_index("dp")
    z = lax.axis_index("layer")
    x, core = me // 2, me % 2

    load = pltpu.make_async_copy(train_hbm, train, train_sem)
    load.start()

    sibling = (y, 2 * x + 1 - core, z)
    across = (1 - y, me, z)
    far = [(y, 2 * ((x + o) % chips) + core, z) for o in range(1, chips)]
    owners = [(y, me, (z + o) % layers) for o in range(1, layers)]

    barrier = pltpu.get_barrier_semaphore()
    others = [sibling, across] + far + owners
    for other in others:
        pl.semaphore_signal(barrier, inc=1, device_id=other, device_id_type=MESH)
    pl.semaphore_wait(barrier, len(others))

    def rows(chunk):
        return pl.ds(chunk * CHUNK, CHUNK)

    started = []
    for chunk in range(chunks):
        for o in range(1, chips):
            source = p_ref.at[
                pl.ds(pl.multiple_of(y * half + chunk * CHUNK, CHUNK), CHUNK), :
            ]
            started.append(
                pltpu.make_async_remote_copy(
                    source,
                    every.at[x, y, core, rows(chunk), :],
                    far_send.at[o, chunk],
                    far_recv.at[o, chunk],
                    device_id=far[o - 1],
                    device_id_type=MESH,
                )
            )
            started[-1].start()
    for h in range(2):
        copy = pltpu.make_async_remote_copy(
            p_ref.at[pl.ds(h * half, half), :],
            every.at[x, h, core],
            core_send.at[0, h, 0],
            core_recv.at[0, h, 0],
            device_id=sibling,
            device_id_type=MESH,
        )
        copy.start()
        started.append(copy)
    for h in range(2):
        every[x, h, core] = p_ref[pl.ds(h * half, half), :]

    def arrived(ref, sem):
        pltpu.make_async_remote_copy(
            ref, ref, sem, sem, device_id=sibling, device_id_type=MESH
        ).wait_recv()

    def forward(chip, h, chunk, send, recv, to):
        block = every.at[chip, h, core, rows(chunk), :]
        copy = pltpu.make_async_remote_copy(
            block, block, send, recv, device_id=to, device_id_type=MESH
        )
        copy.start()
        started.append(copy)

    def unit_sum_copy(chip, h, c):
        block = 2 * chip + c
        place = block % per
        return block // per, place, lambda source: pltpu.make_async_remote_copy(
            ours.at[chip, h, c],
            theirs.at[source, place, h],
            sum_send.at[chip, h, c],
            sum_recv.at[source, place, h],
            device_id=(y, me, block // per),
            device_id_type=MESH,
        )

    tile = min(n, 256)

    def score(chip, hs):
        if len(hs) == 2:
            left_ref = every.at[chip]
        else:
            left_ref = every.at[chip, hs[0]]

        def step(t, carry):
            columns = pl.ds(pl.multiple_of(t * tile, tile), tile)
            left = left_ref[...].reshape(-1, every.shape[-1])
            product = dot_nt(left, train[columns, :])
            for i, h in enumerate(hs):
                for c in range(2):
                    block = 2 * chip + c
                    first = (i * 2 + c) * half
                    piece = product[first : first + half, :]
                    mine = block // per == z

                    @pl.when(mine)
                    def _():
                        start = pl.multiple_of((block % per) * 2 * half + h * half, half)
                        out_ref[pl.ds(start, half), columns] = piece

                    @pl.when(jnp.logical_not(mine))
                    def _():
                        ours[chip, h, c, :, columns] = piece.astype(bf16)

            return carry

        lax.fori_loop(0, n // tile, step, 0)
        for h in hs:
            for c in range(2):
                owner, _, copy = unit_sum_copy(chip, h, c)

                @pl.when(owner != z)
                def _():
                    copy(z).start()

    for h in range(2):
        arrived(every.at[x, h, 1 - core], core_recv.at[0, h, 0])
    load.wait()
    score(x, (0, 1))

    for o in range(1, chips):
        source = (x + chips - o) % chips
        for chunk in range(chunks):
            arrived(every.at[source, y, core, rows(chunk), :], far_recv.at[o, chunk])
            forward(source, y, chunk, row_send.at[o, chunk], row_recv.at[o, chunk], across)
            forward(
                source, y, chunk, core_send.at[o, 0, chunk], core_recv.at[o, 0, chunk], sibling
            )
        for chunk in range(chunks):
            arrived(every.at[source, y, 1 - core, rows(chunk), :], core_recv.at[o, 0, chunk])
        score(source, (y,))
    for o in range(1, chips):
        source = (x + chips - o) % chips
        for chunk in range(chunks):
            arrived(every.at[source, 1 - y, core, rows(chunk), :], row_recv.at[o, chunk])
            forward(
                source,
                1 - y,
                chunk,
                core_send.at[o, 1, chunk],
                core_recv.at[o, 1, chunk],
                sibling,
            )
        for chunk in range(chunks):
            arrived(
                every.at[source, 1 - y, 1 - core, rows(chunk), :], core_recv.at[o, 1, chunk]
            )
        score(source, (1 - y,))

    for place in range(per):
        for h in range(2):
            for o in range(1, layers):
                source = (z + o) % layers
                arrived(theirs.at[source, place, h], sum_recv.at[source, place, h])
            start = (place * 2 + h) * half
            total = out_ref[start : start + half, :]
            for o in range(1, layers):
                total = total + theirs[(z + o) % layers, place, h].astype(f32)
            out_ref[start : start + half, :] = total

    for copy in started:
        copy.wait_send()
    for chip in range(chips):
        for h in range(2):
            for c in range(2):
                if True:
                    owner, _, copy = unit_sum_copy(chip, h, c)

                    @pl.when(owner != z)
                    def _():
                        copy(z).wait_send()


def scores(train_rows, ready, dp, layers):
    n, entries = train_rows.shape
    count = ready.shape[0]
    chips, per, half = dp // 2, dp // layers, count // 2
    chunks = half // CHUNK
    vmem = pl.BlockSpec(memory_space=pltpu.VMEM)
    dma = pltpu.SemaphoreType.DMA
    return pl.pallas_call(
        functools.partial(score_kernel, (dp, layers)),
        out_shape=jax.ShapeDtypeStruct((per * count, n), f32),
        in_specs=[pl.BlockSpec(memory_space=pl.ANY), vmem],
        out_specs=vmem,
        scratch_shapes=[
            pltpu.VMEM((n, entries), bf16),
            pltpu.VMEM((chips, 2, 2, half, entries), bf16),
            pltpu.VMEM((chips, 2, 2, half, n), bf16),
            pltpu.VMEM((layers, per, 2, half, n), bf16),
            dma,
            dma((chips, chunks)),
            dma((chips, chunks)),
            dma((chips, chunks)),
            dma((chips, chunks)),
            dma((chips, 2, chunks)),
            dma((chips, 2, chunks)),
            dma((chips, 2, 2)),
            dma((layers, per, 2)),
        ],
        compiler_params=pltpu.CompilerParams(
            collective_id=0, has_side_effects=True, vmem_limit_bytes=VMEM_LIMIT
        ),
        name="scores",
    )(train_rows, ready)


def solution(mesh):
    dp, layers = mesh.shape["dp"], mesh.shape["layer"]

    def body(train_grads, query_grads, basis_out, basis_in, scaling):
        ready = precondition(query_grads[:, 0, :], basis_out[0], basis_in[0], scaling[0])
        return scores(train_grads[:, 0, :], ready, dp, layers)

    in_specs = (
        P(("groups", "dp"), "layer", None),
        P("dp", "layer", None),
        P("layer", None, None),
        P("layer", None, None),
        P("layer", None, None),
    )
    out_specs = P("layer", ("groups", "dp"))
    return jax.shard_map(body, mesh=mesh, in_specs=in_specs, out_specs=out_specs, check_vma=False)
```

```python
import functools

import jax
import jax.numpy as jnp
from jax import lax
from jax.experimental import pallas as pl
from jax.experimental.pallas import tpu as pltpu
from jax.sharding import PartitionSpec as P

damping = 0.1
f32 = jnp.float32
bf16 = jnp.bfloat16
MESH = pl.DeviceIdType.MESH
VMEM_LIMIT = 56 * 1024 * 1024
NT = (((1,), (1,)), ((), ()))
D = 64
CHUNK = 16


def dot_nt(a, b):
    return lax.dot_general(a, b, NT, preferred_element_type=f32)


def high_low(x):
    high = x.astype(bf16)
    return high, (x - high.astype(f32)).astype(bf16)


def lane_split(x):
    high, low = high_low(x)
    lane = lax.broadcasted_iota(jnp.int32, x.shape, 1)
    return jnp.where((lane // D) % 2 == 0, high.astype(f32), low.astype(f32)).astype(bf16)


def row_split(x):
    high, low = high_low(x)
    return jnp.concatenate([high, high, low, low], axis=0)


def precondition_kernel(
    g_ref, bo_ref, bi_ref, s_ref, p_ref, wide, tall, square, rot, back, bo4, bi4, d4, w_in
):
    count = g_ref.shape[0]
    bo, bi = bo_ref[...], bi_ref[...]
    inverse = 1.0 / (s_ref[...] + damping)

    for j in range(4):
        bo4[:, j * D : (j + 1) * D] = bo
        bi4[:, j * D : (j + 1) * D] = bi
        for i in range(4):
            wide[i * D : (i + 1) * D, j * D : (j + 1) * D] = bo
    lane = lax.broadcasted_iota(jnp.int32, wide.shape, 1)
    high, low = high_low(wide[...])
    wide_split = jnp.where(lane < 2 * D, high.astype(f32), low.astype(f32)).astype(bf16)
    tall[...] = jnp.zeros_like(tall)
    for j in range(4):
        tall[j * D : (j + 1) * D, 0:D] = inverse
    d4[...] = jnp.transpose(tall[...])
    square[...] = jnp.zeros_like(square)
    square[0:D, 0:D] = bi
    square[D : 2 * D, D : 2 * D] = bi
    high, low = high_low(jnp.transpose(square[...]))
    w_in[...] = jnp.concatenate([high, low], axis=1)
    bi4_split = lane_split(bi4[...])

    weights = w_in[...]
    for pair in range(D // 2):
        block = g_ref[:, pair * 2 * D : (pair + 1) * 2 * D]
        rot[pair * 2 * D : (pair + 1) * 2 * D, :] = dot_nt(
            weights, jnp.concatenate([block, block], axis=1)
        )

    bo_four = bo4[...]
    group = 8

    def middle(step, carry):
        first = step * group
        scales = d4[pl.ds(pl.multiple_of(first, group), group), :]
        left = jnp.concatenate(
            [lane_split(bo_four * scales[i : i + 1, :]) for i in range(group)], axis=0
        )
        mats = lane_split(dot_nt(left, wide_split))
        for i in range(group):
            column = rot[pl.ds(first + i, D, stride=D), :]
            back[pl.ds(pl.multiple_of((first + i) * D, D), D), :] = jnp.dot(
                mats[i * D : (i + 1) * D, :], row_split(column), preferred_element_type=f32
            )
        return carry

    lax.fori_loop(0, D // group, middle, 0)

    for pair in range(D // 2):
        halves = [
            jnp.dot(
                bi4_split,
                row_split(back[pl.ds(2 * pair + i, D, stride=D), :]),
                preferred_element_type=f32,
            )
            for i in range(2)
        ]
        block = jnp.transpose(jnp.concatenate(halves, axis=0))
        p_ref[:, pair * 2 * D : (pair + 1) * 2 * D] = block.astype(bf16)


def precondition(grads, bo, bi, s):
    count, entries = grads.shape
    vmem = pl.BlockSpec(memory_space=pltpu.VMEM)
    return pl.pallas_call(
        precondition_kernel,
        out_shape=jax.ShapeDtypeStruct((count, entries), bf16),
        in_specs=[vmem] * 4,
        out_specs=vmem,
        scratch_shapes=[
            pltpu.VMEM((4 * D, 4 * D), f32),
            pltpu.VMEM((4 * D, 2 * D), f32),
            pltpu.VMEM((2 * D, 2 * D), f32),
            pltpu.VMEM((entries, count), f32),
            pltpu.VMEM((entries, count), f32),
            pltpu.VMEM((D, 4 * D), f32),
            pltpu.VMEM((D, 4 * D), f32),
            pltpu.VMEM((2 * D, 4 * D), f32),
            pltpu.VMEM((2 * D, 4 * D), bf16),
        ],
        compiler_params=pltpu.CompilerParams(vmem_limit_bytes=VMEM_LIMIT),
        name="precondition",
    )(grads, bo, bi, s)


def score_kernel(
    sizes,
    train_hbm,
    p_ref,
    out_ref,
    train,
    every,
    exact,
    ours,
    relay,
    theirs,
    train_sem,
    far_send,
    far_recv,
    row_send,
    row_recv,
    core_send,
    core_recv,
    sum_send,
    sum_recv,
    relay_recv,
):
    dp, layers = sizes
    chips = dp // 2
    per = dp // layers
    half = p_ref.shape[0] // 2
    chunks = half // CHUNK
    n = train.shape[0]
    y = lax.axis_index("groups")
    me = lax.axis_index("dp")
    z = lax.axis_index("layer")
    x, core = me // 2, me % 2

    load = pltpu.make_async_copy(train_hbm, train, train_sem)
    load.start()

    sibling = (y, 2 * x + 1 - core, z)
    across = (1 - y, me, z)
    far = [(y, 2 * ((x + o) % chips) + core, z) for o in range(1, chips)]
    owners = [(y, me, (z + o) % layers) for o in range(1, layers)]

    barrier = pltpu.get_barrier_semaphore()
    others = [sibling, across] + far + owners
    for other in others:
        pl.semaphore_signal(barrier, inc=1, device_id=other, device_id_type=MESH)
    pl.semaphore_wait(barrier, len(others))

    def rows(chunk):
        return pl.ds(chunk * CHUNK, CHUNK)

    started = []
    for chunk in range(chunks):
        for o in range(1, chips):
            source = p_ref.at[
                pl.ds(pl.multiple_of(y * half + chunk * CHUNK, CHUNK), CHUNK), :
            ]
            started.append(
                pltpu.make_async_remote_copy(
                    source,
                    every.at[x, y, core, rows(chunk), :],
                    far_send.at[o, chunk],
                    far_recv.at[o, chunk],
                    device_id=far[o - 1],
                    device_id_type=MESH,
                )
            )
            started[-1].start()
    for h in range(2):
        copy = pltpu.make_async_remote_copy(
            p_ref.at[pl.ds(h * half, half), :],
            every.at[x, h, core],
            core_send.at[0, h, 0],
            core_recv.at[0, h, 0],
            device_id=sibling,
            device_id_type=MESH,
        )
        copy.start()
        started.append(copy)
    for h in range(2):
        every[x, h, core] = p_ref[pl.ds(h * half, half), :]

    def arrived(ref, sem):
        pltpu.make_async_remote_copy(
            ref, ref, sem, sem, device_id=sibling, device_id_type=MESH
        ).wait_recv()

    def forward(chip, h, chunk, send, recv, to):
        block = every.at[chip, h, core, rows(chunk), :]
        copy = pltpu.make_async_remote_copy(
            block, block, send, recv, device_id=to, device_id_type=MESH
        )
        copy.start()
        started.append(copy)

    partner = z + 1 - 2 * (z % 2)

    def route(chip, h, c):
        block = 2 * chip + c
        owner, place = block // per, block % per
        inside = owner // 2 == z // 2
        upward = owner > z
        near = jnp.logical_not(inside) & (upward == (z % 2 == 1))
        direct = inside & (owner != z)
        outer = jnp.logical_not(inside) & (upward != (z % 2 == 1))
        return owner, place, direct, outer, near

    def sum_copy(chip, h, c):
        owner, place, _, _, _ = route(chip, h, c)
        return pltpu.make_async_remote_copy(
            ours.at[chip, h, c],
            theirs.at[z // 2, place, h],
            sum_send.at[chip, h, c],
            sum_recv.at[z // 2, place, h],
            device_id=(y, me, owner),
            device_id_type=MESH,
        )

    def relay_copy(chip, h, c):
        return pltpu.make_async_remote_copy(
            ours.at[chip, h, c],
            relay.at[chip, h, c],
            sum_send.at[chip, h, c],
            relay_recv.at[chip, h, c],
            device_id=(y, me, partner),
            device_id_type=MESH,
        )

    def send_sums(chip, hs):
        for h in hs:
            for c in range(2):
                _, _, direct, outer, _ = route(chip, h, c)

                @pl.when(outer)
                def _():
                    relay_copy(chip, h, c).start()

                @pl.when(direct)
                def _():
                    sum_copy(chip, h, c).start()

    def combine(chip, h, c):
        _, _, _, _, near = route(chip, h, c)

        @pl.when(near)
        def _():
            relay_copy(chip, h, c).wait_recv()
            ours[chip, h, c] = (exact[chip, h, c] + relay[chip, h, c].astype(f32)).astype(bf16)
            sum_copy(chip, h, c).start()

    tile = min(n, 256)

    def score_tile(chip, hs, t):
        columns = pl.ds(pl.multiple_of(t * tile, tile), tile)
        left = every[chip] if len(hs) == 2 else every[chip, hs[0]]
        product = dot_nt(left.reshape(-1, every.shape[-1]), train[columns, :])
        for i, h in enumerate(hs):
            for c in range(2):
                first = (i * 2 + c) * half
                piece = product[first : first + half, :]
                exact[chip, h, c, :, columns] = piece
                ours[chip, h, c, :, columns] = piece.astype(bf16)

    def score(chip, hs):
        def step(t, carry):
            score_tile(chip, hs, t)
            return carry

        lax.fori_loop(0, n // tile, step, 0)
        send_sums(chip, hs)

    for h in range(2):
        arrived(every.at[x, h, 1 - core], core_recv.at[0, h, 0])
    load.wait()
    def pass_on(chunk):
        for o in range(1, chips):
            source = (x + chips - o) % chips
            arrived(every.at[source, y, core, rows(chunk), :], far_recv.at[o, chunk])
            forward(source, y, chunk, row_send.at[o, chunk], row_recv.at[o, chunk], across)
            forward(
                source, y, chunk, core_send.at[o, 0, chunk], core_recv.at[o, 0, chunk], sibling
            )

    passed = 0
    for t in range(n // tile):
        score_tile(x, (0, 1), t)
        if passed < chunks and t < n // tile - 1:
            pass_on(passed)
            passed += 1
    send_sums(x, (0, 1))
    for chunk in range(passed, chunks):
        pass_on(chunk)
    for o in range(1, chips):
        source = (x + chips - o) % chips
        for chunk in range(chunks):
            arrived(every.at[source, y, 1 - core, rows(chunk), :], core_recv.at[o, 0, chunk])
        score(source, (y,))
    pieces = [(h, c) for h in range(2) for c in range(2)]
    for o in range(1, chips):
        source = (x + chips - o) % chips
        for chunk in range(chunks):
            arrived(every.at[source, 1 - y, core, rows(chunk), :], row_recv.at[o, chunk])
            forward(
                source,
                1 - y,
                chunk,
                core_send.at[o, 1, chunk],
                core_recv.at[o, 1, chunk],
                sibling,
            )
            if o == 1 and chunk < len(pieces):
                combine(x, *pieces[chunk])
        if o == 1:
            for h, c in pieces[chunks:]:
                combine(x, h, c)
        for chunk in range(chunks):
            arrived(
                every.at[source, 1 - y, 1 - core, rows(chunk), :], core_recv.at[o, 1, chunk]
            )
        score(source, (1 - y,))
    for o in range(1, chips):
        source = (x + chips - o) % chips
        for h in (y, 1 - y):
            for c in range(2):
                combine(source, h, c)

    pairs = layers // 2
    for place in range(per):
        block = z * per + place
        for h in range(2):
            for o in range(pairs):
                source = (z // 2 + o) % pairs
                arrived(theirs.at[source, place, h], sum_recv.at[source, place, h])
            total = exact[block // 2, h, block % 2]
            for o in range(pairs):
                total = total + theirs[(z // 2 + o) % pairs, place, h].astype(f32)
            start = (place * 2 + h) * half
            out_ref[start : start + half, :] = total

    for copy in started:
        copy.wait_send()
    for chip in range(chips):
        for h, c in pieces:
            owner, _, _, _, _ = route(chip, h, c)

            @pl.when(owner != z)
            def _():
                relay_copy(chip, h, c).wait_send()


def scores(train_rows, ready, dp, layers):
    n, entries = train_rows.shape
    count = ready.shape[0]
    chips, per, half = dp // 2, dp // layers, count // 2
    chunks = half // CHUNK
    vmem = pl.BlockSpec(memory_space=pltpu.VMEM)
    dma = pltpu.SemaphoreType.DMA
    return pl.pallas_call(
        functools.partial(score_kernel, (dp, layers)),
        out_shape=jax.ShapeDtypeStruct((per * count, n), f32),
        in_specs=[pl.BlockSpec(memory_space=pl.ANY), vmem],
        out_specs=vmem,
        scratch_shapes=[
            pltpu.VMEM((n, entries), bf16),
            pltpu.VMEM((chips, 2, 2, half, entries), bf16),
            pltpu.VMEM((chips, 2, 2, half, n), f32),
            pltpu.VMEM((chips, 2, 2, half, n), bf16),
            pltpu.VMEM((chips, 2, 2, half, n), bf16),
            pltpu.VMEM((layers // 2, per, 2, half, n), bf16),
            dma,
            dma((chips, chunks)),
            dma((chips, chunks)),
            dma((chips, chunks)),
            dma((chips, chunks)),
            dma((chips, 2, chunks)),
            dma((chips, 2, chunks)),
            dma((chips, 2, 2)),
            dma((layers // 2, per, 2)),
            dma((chips, 2, 2)),
        ],
        compiler_params=pltpu.CompilerParams(
            collective_id=0, has_side_effects=True, vmem_limit_bytes=VMEM_LIMIT
        ),
        name="scores",
    )(train_rows, ready)


def solution(mesh):
    dp, layers = mesh.shape["dp"], mesh.shape["layer"]

    def body(train_grads, query_grads, basis_out, basis_in, scaling):
        ready = precondition(query_grads[:, 0, :], basis_out[0], basis_in[0], scaling[0])
        return scores(train_grads[:, 0, :], ready, dp, layers)

    in_specs = (
        P(("groups", "dp"), "layer", None),
        P("dp", "layer", None),
        P("layer", None, None),
        P("layer", None, None),
        P("layer", None, None),
    )
    out_specs = P("layer", ("groups", "dp"))
    return jax.shard_map(body, mesh=mesh, in_specs=in_specs, out_specs=out_specs, check_vma=False)
```

```python
import functools

import jax
import jax.numpy as jnp
from jax import lax
from jax.experimental import pallas as pl
from jax.experimental.pallas import tpu as pltpu
from jax.sharding import PartitionSpec as P

damping = 0.1
f32 = jnp.float32
bf16 = jnp.bfloat16
MESH = pl.DeviceIdType.MESH
VMEM_LIMIT = 56 * 1024 * 1024
NT = (((1,), (1,)), ((), ()))
D = 64
CHUNKS = 8


def dot_nt(a, b):
    return lax.dot_general(a, b, NT, preferred_element_type=f32)


def high_low(x):
    high = x.astype(bf16)
    return high, (x - high.astype(f32)).astype(bf16)


def lane_split(x):
    high, low = high_low(x)
    lane = lax.broadcasted_iota(jnp.int32, x.shape, 1)
    return jnp.where((lane // D) % 2 == 0, high.astype(f32), low.astype(f32)).astype(bf16)


def row_split(x):
    high, low = high_low(x)
    return jnp.concatenate([high, high, low, low], axis=0)


def precondition_rows(
    g_ref, bo_ref, bi_ref, s_ref, scratch, put, finished
):
    wide, tall, square, rot, back, bo4, bi4, d4, w_in = scratch
    bo, bi = bo_ref[...], bi_ref[...]
    inverse = 1.0 / (s_ref[...] + damping)

    for j in range(4):
        bo4[:, j * D : (j + 1) * D] = bo
        bi4[:, j * D : (j + 1) * D] = bi
        for i in range(4):
            wide[i * D : (i + 1) * D, j * D : (j + 1) * D] = bo
    lane = lax.broadcasted_iota(jnp.int32, wide.shape, 1)
    high, low = high_low(wide[...])
    wide_split = jnp.where(lane < 2 * D, high.astype(f32), low.astype(f32)).astype(bf16)
    tall[...] = jnp.zeros_like(tall)
    for j in range(4):
        tall[j * D : (j + 1) * D, 0:D] = inverse
    d4[...] = jnp.transpose(tall[...])
    square[...] = jnp.zeros_like(square)
    square[0:D, 0:D] = bi
    square[D : 2 * D, D : 2 * D] = bi
    high, low = high_low(jnp.transpose(square[...]))
    w_in[...] = jnp.concatenate([high, low], axis=1)
    bi4_split = lane_split(bi4[...])

    weights = w_in[...]
    for pair in range(D // 2):
        block = g_ref[:, pair * 2 * D : (pair + 1) * 2 * D]
        rot[pair * 2 * D : (pair + 1) * 2 * D, :] = dot_nt(
            weights, jnp.concatenate([block, block], axis=1)
        )

    bo_four = bo4[...]
    group = 8

    def middle(step, carry):
        first = step * group
        scales = d4[pl.ds(pl.multiple_of(first, group), group), :]
        left = jnp.concatenate(
            [lane_split(bo_four * scales[i : i + 1, :]) for i in range(group)], axis=0
        )
        mats = lane_split(dot_nt(left, wide_split))
        for i in range(group):
            column = rot[pl.ds(first + i, D, stride=D), :]
            back[pl.ds(pl.multiple_of((first + i) * D, D), D), :] = jnp.dot(
                mats[i * D : (i + 1) * D, :], row_split(column), preferred_element_type=f32
            )
        return carry

    lax.fori_loop(0, D // group, middle, 0)

    for pair in range(D // 2):
        halves = [
            jnp.dot(
                bi4_split,
                row_split(back[pl.ds(2 * pair + i, D, stride=D), :]),
                preferred_element_type=f32,
            )
            for i in range(2)
        ]
        block = jnp.transpose(jnp.concatenate(halves, axis=0))
        put(pair * 2 * D, block.astype(bf16))
        if (pair + 1) % (D // 2 // CHUNKS) == 0:
            finished((pair + 1) // (D // 2 // CHUNKS) - 1)


def score_kernel(
    sizes,
    train_hbm,
    g_ref,
    bo_ref,
    bi_ref,
    s_ref,
    out_ref,
    train,
    every,
    exact,
    ours,
    relay,
    theirs,
    train_sem,
    far_send,
    far_recv,
    row_send,
    row_recv,
    core_send,
    core_recv,
    sum_send,
    sum_recv,
    relay_recv,
    *scratch,
):
    dp, layers = sizes
    chips = dp // 2
    per = dp // layers
    half = g_ref.shape[0] // 2
    width = g_ref.shape[1] // CHUNKS
    n = train.shape[0]
    y = lax.axis_index("groups")
    me = lax.axis_index("dp")
    z = lax.axis_index("layer")
    x, core = me // 2, me % 2

    load = pltpu.make_async_copy(train_hbm, train, train_sem)
    load.start()

    sibling = (y, 2 * x + 1 - core, z)
    across = (1 - y, me, z)
    far = [(y, 2 * ((x + o) % chips) + core, z) for o in range(1, chips)]
    owners = [(y, me, (z + o) % layers) for o in range(1, layers)]

    barrier = pltpu.get_barrier_semaphore()
    others = [sibling, across] + far + owners
    for other in others:
        pl.semaphore_signal(barrier, inc=1, device_id=other, device_id_type=MESH)

    started = []

    def part(chip, h, c, chunk):
        return every.at[chip, h, c, :, pl.ds(chunk * width, width)]

    def send(chip, h, chunk, send_sem, recv_sem, to):
        block = part(chip, h, core, chunk)
        copy = pltpu.make_async_remote_copy(
            block, block, send_sem, recv_sem, device_id=to, device_id_type=MESH
        )
        copy.start()
        started.append(copy)

    def put(first, block):
        for h in range(2):
            every[x, h, core, :, first : first + 2 * D] = block[h * half : (h + 1) * half, :]

    def finished(chunk):
        if chunk == 0:
            pl.semaphore_wait(barrier, len(others))
        for o in range(1, chips):
            send(x, y, chunk, far_send.at[o, chunk], far_recv.at[o, chunk], far[o - 1])
        for h in range(2):
            send(x, h, chunk, core_send.at[0, h, chunk], core_recv.at[0, h, chunk], sibling)

    precondition_rows(g_ref, bo_ref, bi_ref, s_ref, scratch, put, finished)

    def arrived(ref, sem):
        pltpu.make_async_remote_copy(
            ref, ref, sem, sem, device_id=sibling, device_id_type=MESH
        ).wait_recv()

    partner = z + 1 - 2 * (z % 2)

    def route(chip, h, c):
        block = 2 * chip + c
        owner, place = block // per, block % per
        inside = owner // 2 == z // 2
        upward = owner > z
        near = jnp.logical_not(inside) & (upward == (z % 2 == 1))
        direct = inside & (owner != z)
        outer = jnp.logical_not(inside) & (upward != (z % 2 == 1))
        return owner, place, direct, outer, near

    def sum_copy(chip, h, c):
        owner, place, _, _, _ = route(chip, h, c)
        return pltpu.make_async_remote_copy(
            ours.at[chip, h, c],
            theirs.at[z // 2, place, h],
            sum_send.at[chip, h, c],
            sum_recv.at[z // 2, place, h],
            device_id=(y, me, owner),
            device_id_type=MESH,
        )

    def relay_copy(chip, h, c):
        return pltpu.make_async_remote_copy(
            ours.at[chip, h, c],
            relay.at[chip, h, c],
            sum_send.at[chip, h, c],
            relay_recv.at[chip, h, c],
            device_id=(y, me, partner),
            device_id_type=MESH,
        )

    def send_sums(chip, hs):
        for h in hs:
            for c in range(2):
                _, _, direct, outer, _ = route(chip, h, c)

                @pl.when(outer)
                def _():
                    relay_copy(chip, h, c).start()

                @pl.when(direct)
                def _():
                    sum_copy(chip, h, c).start()

    def combine(chip, h, c):
        _, _, _, _, near = route(chip, h, c)

        @pl.when(near)
        def _():
            relay_copy(chip, h, c).wait_recv()
            ours[chip, h, c] = (exact[chip, h, c] + relay[chip, h, c].astype(f32)).astype(bf16)
            sum_copy(chip, h, c).start()

    tile = min(n, 256)

    def score(chip, hs, chunk):
        depth = pl.ds(chunk * width, width)

        def step(t, carry):
            columns = pl.ds(pl.multiple_of(t * tile, tile), tile)
            if len(hs) == 2:
                left = every[chip, :, :, :, depth]
            else:
                left = every[chip, hs[0], :, :, depth]
            product = dot_nt(left.reshape(-1, width), train[columns, depth])
            for i, h in enumerate(hs):
                for c in range(2):
                    first = (i * 2 + c) * half
                    piece = product[first : first + half, :]
                    if chunk > 0:
                        piece = piece + exact[chip, h, c, :, columns]
                    exact[chip, h, c, :, columns] = piece
                    if chunk == CHUNKS - 1:
                        ours[chip, h, c, :, columns] = piece.astype(bf16)
            return carry

        lax.fori_loop(0, n // tile, step, 0)
        if chunk == CHUNKS - 1:
            send_sums(chip, hs)

    def pass_on(o, chunk):
        source = (x + chips - o) % chips
        arrived(part(source, y, core, chunk), far_recv.at[o, chunk])
        send(source, y, chunk, row_send.at[o, chunk], row_recv.at[o, chunk], across)
        send(source, y, chunk, core_send.at[o, 0, chunk], core_recv.at[o, 0, chunk], sibling)

    load.wait()
    passed = 0
    for chunk in range(CHUNKS):
        for h in range(2):
            arrived(part(x, h, 1 - core, chunk), core_recv.at[0, h, chunk])
        score(x, (0, 1), chunk)
        if chunk % 2 == 1:
            pass_on(1, passed)
            passed += 1
    for o in range(1, chips):
        source = (x + chips - o) % chips
        for chunk in range(CHUNKS):
            if o > 1 or chunk >= passed:
                pass_on(o, chunk)
            if chunk > 0:
                arrived(part(source, y, 1 - core, chunk - 1), core_recv.at[o, 0, chunk - 1])
                score(source, (y,), chunk - 1)
        last = CHUNKS - 1
        arrived(part(source, y, 1 - core, last), core_recv.at[o, 0, last])
        score(source, (y,), last)
    pieces = [(h, c) for h in range(2) for c in range(2)]
    for o in range(1, chips):
        source = (x + chips - o) % chips
        for chunk in range(CHUNKS + 1):
            if chunk < CHUNKS:
                arrived(part(source, 1 - y, core, chunk), row_recv.at[o, chunk])
                send(
                    source,
                    1 - y,
                    chunk,
                    core_send.at[o, 1, chunk],
                    core_recv.at[o, 1, chunk],
                    sibling,
                )
            if chunk > 0:
                arrived(
                    part(source, 1 - y, 1 - core, chunk - 1), core_recv.at[o, 1, chunk - 1]
                )
                score(source, (1 - y,), chunk - 1)
    for h, c in pieces:
        combine(x, h, c)
    for o in range(1, chips):
        source = (x + chips - o) % chips
        for h in (y, 1 - y):
            for c in range(2):
                combine(source, h, c)

    pairs = layers // 2
    for place in range(per):
        block = z * per + place
        for h in range(2):
            for o in range(pairs):
                source = (z // 2 + o) % pairs
                arrived(theirs.at[source, place, h], sum_recv.at[source, place, h])
            total = exact[block // 2, h, block % 2]
            for o in range(pairs):
                total = total + theirs[(z // 2 + o) % pairs, place, h].astype(f32)
            start = (place * 2 + h) * half
            out_ref[start : start + half, :] = total

    for copy in started:
        copy.wait_send()
    for chip in range(chips):
        for h, c in pieces:
            owner, _, _, _, _ = route(chip, h, c)

            @pl.when(owner != z)
            def _():
                relay_copy(chip, h, c).wait_send()


def scores(train_rows, grads, bo, bi, s, dp, layers):
    n, entries = train_rows.shape
    count = grads.shape[0]
    chips, per, half = dp // 2, dp // layers, count // 2
    chunks = CHUNKS
    vmem = pl.BlockSpec(memory_space=pltpu.VMEM)
    dma = pltpu.SemaphoreType.DMA
    return pl.pallas_call(
        functools.partial(score_kernel, (dp, layers)),
        out_shape=jax.ShapeDtypeStruct((per * count, n), f32),
        in_specs=[pl.BlockSpec(memory_space=pl.ANY)] + [vmem] * 4,
        out_specs=vmem,
        scratch_shapes=[
            pltpu.VMEM((n, entries), bf16),
            pltpu.VMEM((chips, 2, 2, half, entries), bf16),
            pltpu.VMEM((chips, 2, 2, half, n), f32),
            pltpu.VMEM((chips, 2, 2, half, n), bf16),
            pltpu.VMEM((chips, 2, 2, half, n), bf16),
            pltpu.VMEM((layers // 2, per, 2, half, n), bf16),
            dma,
            dma((chips, chunks)),
            dma((chips, chunks)),
            dma((chips, chunks)),
            dma((chips, chunks)),
            dma((chips, 2, chunks)),
            dma((chips, 2, chunks)),
            dma((chips, 2, 2)),
            dma((layers // 2, per, 2)),
            dma((chips, 2, 2)),
            pltpu.VMEM((4 * D, 4 * D), f32),
            pltpu.VMEM((4 * D, 2 * D), f32),
            pltpu.VMEM((2 * D, 2 * D), f32),
            pltpu.VMEM((entries, count), f32),
            pltpu.VMEM((entries, count), f32),
            pltpu.VMEM((D, 4 * D), f32),
            pltpu.VMEM((D, 4 * D), f32),
            pltpu.VMEM((2 * D, 4 * D), f32),
            pltpu.VMEM((2 * D, 4 * D), bf16),
        ],
        compiler_params=pltpu.CompilerParams(
            collective_id=0, has_side_effects=True, vmem_limit_bytes=VMEM_LIMIT
        ),
        name="scores",
    )(train_rows, grads, bo, bi, s)


def solution(mesh):
    dp, layers = mesh.shape["dp"], mesh.shape["layer"]

    def body(train_grads, query_grads, basis_out, basis_in, scaling):
        return scores(
            train_grads[:, 0, :],
            query_grads[:, 0, :],
            basis_out[0],
            basis_in[0],
            scaling[0],
            dp,
            layers,
        )

    in_specs = (
        P(("groups", "dp"), "layer", None),
        P("dp", "layer", None),
        P("layer", None, None),
        P("layer", None, None),
        P("layer", None, None),
    )
    out_specs = P("layer", ("groups", "dp"))
    return jax.shard_map(body, mesh=mesh, in_specs=in_specs, out_specs=out_specs, check_vma=False)
```

```python
import functools

import jax
import jax.numpy as jnp
from jax import lax
from jax.experimental import pallas as pl
from jax.experimental.pallas import tpu as pltpu
from jax.sharding import PartitionSpec as P

damping = 0.1
f32 = jnp.float32
bf16 = jnp.bfloat16
MESH = pl.DeviceIdType.MESH
VMEM_LIMIT = 56 * 1024 * 1024
NT = (((1,), (1,)), ((), ()))
D = 64
CHUNKS = 8


def dot_nt(a, b):
    return lax.dot_general(a, b, NT, preferred_element_type=f32)


def high_low(x):
    high = x.astype(bf16)
    return high, (x - high.astype(f32)).astype(bf16)


def lane_split(x):
    high, low = high_low(x)
    lane = lax.broadcasted_iota(jnp.int32, x.shape, 1)
    return jnp.where((lane // D) % 2 == 0, high.astype(f32), low.astype(f32)).astype(bf16)


def row_split(x):
    high, low = high_low(x)
    return jnp.concatenate([high, high, low, low], axis=0)


def precondition_rows(
    g_ref, bo_ref, bi_ref, s_ref, scratch, put, finished
):
    wide, tall, square, rot, back, bo4, bi4, d4, w_in = scratch
    bo, bi = bo_ref[...], bi_ref[...]
    inverse = 1.0 / (s_ref[...] + damping)

    for j in range(4):
        bo4[:, j * D : (j + 1) * D] = bo
        bi4[:, j * D : (j + 1) * D] = bi
        for i in range(4):
            wide[i * D : (i + 1) * D, j * D : (j + 1) * D] = bo
    lane = lax.broadcasted_iota(jnp.int32, wide.shape, 1)
    high, low = high_low(wide[...])
    wide_split = jnp.where(lane < 2 * D, high.astype(f32), low.astype(f32)).astype(bf16)
    tall[...] = jnp.zeros_like(tall)
    for j in range(4):
        tall[j * D : (j + 1) * D, 0:D] = inverse
    d4[...] = jnp.transpose(tall[...])
    square[...] = jnp.zeros_like(square)
    square[0:D, 0:D] = bi
    square[D : 2 * D, D : 2 * D] = bi
    high, low = high_low(jnp.transpose(square[...]))
    w_in[...] = jnp.concatenate([high, low], axis=1)
    bi4_split = lane_split(bi4[...])

    weights = w_in[...]
    for pair in range(D // 2):
        block = g_ref[:, pair * 2 * D : (pair + 1) * 2 * D]
        rot[pair * 2 * D : (pair + 1) * 2 * D, :] = dot_nt(
            weights, jnp.concatenate([block, block], axis=1)
        )

    bo_four = bo4[...]
    group = 8

    def middle(step, carry):
        first = step * group
        scales = d4[pl.ds(pl.multiple_of(first, group), group), :]
        left = jnp.concatenate(
            [lane_split(bo_four * scales[i : i + 1, :]) for i in range(group)], axis=0
        )
        mats = lane_split(dot_nt(left, wide_split))
        for i in range(group):
            column = rot[pl.ds(first + i, D, stride=D), :]
            back[pl.ds(pl.multiple_of((first + i) * D, D), D), :] = jnp.dot(
                mats[i * D : (i + 1) * D, :], row_split(column), preferred_element_type=f32
            )
        return carry

    lax.fori_loop(0, D // group, middle, 0)

    for pair in range(D // 2):
        halves = [
            jnp.dot(
                bi4_split,
                row_split(back[pl.ds(2 * pair + i, D, stride=D), :]),
                preferred_element_type=f32,
            )
            for i in range(2)
        ]
        block = jnp.transpose(jnp.concatenate(halves, axis=0))
        put(pair * 2 * D, block.astype(bf16))
        if (pair + 1) % (D // 2 // CHUNKS) == 0:
            finished((pair + 1) // (D // 2 // CHUNKS) - 1)


def score_kernel(
    sizes,
    train_hbm,
    g_ref,
    bo_ref,
    bi_ref,
    s_ref,
    out_ref,
    train,
    every,
    exact,
    ours,
    relay,
    theirs,
    train_sem,
    far_send,
    far_recv,
    row_send,
    row_recv,
    core_send,
    core_recv,
    sum_send,
    sum_recv,
    relay_recv,
    *scratch,
):
    dp, layers = sizes
    chips = dp // 2
    per = dp // layers
    half = g_ref.shape[0] // 2
    width = g_ref.shape[1] // CHUNKS
    n = train.shape[0]
    y = lax.axis_index("groups")
    me = lax.axis_index("dp")
    z = lax.axis_index("layer")
    x, core = me // 2, me % 2

    load = pltpu.make_async_copy(train_hbm, train, train_sem)
    load.start()

    sibling = (y, 2 * x + 1 - core, z)
    across = (1 - y, me, z)
    far = [(y, 2 * ((x + o) % chips) + core, z) for o in range(1, chips)]
    owners = [(y, me, (z + o) % layers) for o in range(1, layers)]

    barrier = pltpu.get_barrier_semaphore()
    others = [sibling, across] + far + owners
    for other in others:
        pl.semaphore_signal(barrier, inc=1, device_id=other, device_id_type=MESH)

    started = []

    def part(chip, h, c, chunk):
        return every.at[chip, h, c, :, pl.ds(chunk * width, width)]

    def send(chip, h, chunk, send_sem, recv_sem, to):
        block = part(chip, h, core, chunk)
        copy = pltpu.make_async_remote_copy(
            block, block, send_sem, recv_sem, device_id=to, device_id_type=MESH
        )
        copy.start()
        started.append(copy)

    def put(first, block):
        for h in range(2):
            every[x, h, core, :, first : first + 2 * D] = block[h * half : (h + 1) * half, :]

    def finished(chunk):
        if chunk == 0:
            pl.semaphore_wait(barrier, len(others))
        for o in range(1, chips):
            send(x, y, chunk, far_send.at[o, chunk], far_recv.at[o, chunk], far[o - 1])
        for h in range(2):
            send(x, h, chunk, core_send.at[0, h, chunk], core_recv.at[0, h, chunk], sibling)

    precondition_rows(g_ref, bo_ref, bi_ref, s_ref, scratch, put, finished)

    def arrived(ref, sem):
        pltpu.make_async_remote_copy(
            ref, ref, sem, sem, device_id=sibling, device_id_type=MESH
        ).wait_recv()

    partner = z + 1 - 2 * (z % 2)

    def route(chip, h, c):
        block = 2 * chip + c
        owner, place = block // per, block % per
        inside = owner // 2 == z // 2
        upward = owner > z
        near = jnp.logical_not(inside) & (upward == (z % 2 == 1))
        direct = inside & (owner != z)
        outer = jnp.logical_not(inside) & (upward != (z % 2 == 1))
        return owner, place, direct, outer, near

    def sum_copy(chip, h, c):
        owner, place, _, _, _ = route(chip, h, c)
        return pltpu.make_async_remote_copy(
            ours.at[chip, h, c],
            theirs.at[z // 2, place, h],
            sum_send.at[chip, h, c],
            sum_recv.at[z // 2, place, h],
            device_id=(y, me, owner),
            device_id_type=MESH,
        )

    def relay_copy(chip, h, c):
        return pltpu.make_async_remote_copy(
            ours.at[chip, h, c],
            relay.at[chip, h, c],
            sum_send.at[chip, h, c],
            relay_recv.at[chip, h, c],
            device_id=(y, me, partner),
            device_id_type=MESH,
        )

    def send_sums(chip, hs):
        for h in hs:
            for c in range(2):
                _, _, direct, outer, _ = route(chip, h, c)

                @pl.when(outer)
                def _():
                    relay_copy(chip, h, c).start()

                @pl.when(direct)
                def _():
                    sum_copy(chip, h, c).start()

    def combine(chip, h, c):
        _, _, _, _, near = route(chip, h, c)

        @pl.when(near)
        def _():
            relay_copy(chip, h, c).wait_recv()
            ours[chip, h, c] = (exact[chip, h, c] + relay[chip, h, c].astype(f32)).astype(bf16)
            sum_copy(chip, h, c).start()

    tile = min(n, 256)

    def score_tile(chip, hs, t):
        columns = pl.ds(pl.multiple_of(t * tile, tile), tile)
        left = every[chip] if len(hs) == 2 else every[chip, hs[0]]
        product = dot_nt(left.reshape(-1, every.shape[-1]), train[columns, :])
        for i, h in enumerate(hs):
            for c in range(2):
                first = (i * 2 + c) * half
                piece = product[first : first + half, :]
                exact[chip, h, c, :, columns] = piece
                ours[chip, h, c, :, columns] = piece.astype(bf16)

    def score(chip, hs):
        def step(t, carry):
            score_tile(chip, hs, t)
            return carry

        lax.fori_loop(0, n // tile, step, 0)
        send_sums(chip, hs)

    def pass_on(o, chunk):
        source = (x + chips - o) % chips
        arrived(part(source, y, core, chunk), far_recv.at[o, chunk])
        send(source, y, chunk, row_send.at[o, chunk], row_recv.at[o, chunk], across)
        send(source, y, chunk, core_send.at[o, 0, chunk], core_recv.at[o, 0, chunk], sibling)

    load.wait()
    for chunk in range(CHUNKS):
        for h in range(2):
            arrived(part(x, h, 1 - core, chunk), core_recv.at[0, h, chunk])
    passed = 0
    for t in range(n // tile):
        score_tile(x, (0, 1), t)
        while passed < min(CHUNKS, 2 * (t + 1)) and t < n // tile - 1:
            pass_on(1, passed)
            passed += 1
    send_sums(x, (0, 1))
    for o in range(1, chips):
        source = (x + chips - o) % chips
        for chunk in range(passed if o == 1 else 0, CHUNKS):
            pass_on(o, chunk)
        for chunk in range(CHUNKS):
            arrived(part(source, y, 1 - core, chunk), core_recv.at[o, 0, chunk])
        score(source, (y,))
    pieces = [(h, c) for h in range(2) for c in range(2)]
    for o in range(1, chips):
        source = (x + chips - o) % chips
        for chunk in range(CHUNKS):
            arrived(part(source, 1 - y, core, chunk), row_recv.at[o, chunk])
            send(
                source,
                1 - y,
                chunk,
                core_send.at[o, 1, chunk],
                core_recv.at[o, 1, chunk],
                sibling,
            )
            if o == 1 and chunk % 2 == 1:
                combine(x, *pieces[chunk // 2])
        for chunk in range(CHUNKS):
            arrived(part(source, 1 - y, 1 - core, chunk), core_recv.at[o, 1, chunk])
        score(source, (1 - y,))
    for o in range(1, chips):
        source = (x + chips - o) % chips
        for h in (y, 1 - y):
            for c in range(2):
                combine(source, h, c)

    pairs = layers // 2
    for place in range(per):
        block = z * per + place
        for h in range(2):
            for o in range(pairs):
                source = (z // 2 + o) % pairs
                arrived(theirs.at[source, place, h], sum_recv.at[source, place, h])
            total = exact[block // 2, h, block % 2]
            for o in range(pairs):
                total = total + theirs[(z // 2 + o) % pairs, place, h].astype(f32)
            start = (place * 2 + h) * half
            out_ref[start : start + half, :] = total

    for copy in started:
        copy.wait_send()
    for chip in range(chips):
        for h, c in pieces:
            owner, _, _, _, _ = route(chip, h, c)

            @pl.when(owner != z)
            def _():
                relay_copy(chip, h, c).wait_send()


def scores(train_rows, grads, bo, bi, s, dp, layers):
    n, entries = train_rows.shape
    count = grads.shape[0]
    chips, per, half = dp // 2, dp // layers, count // 2
    chunks = CHUNKS
    vmem = pl.BlockSpec(memory_space=pltpu.VMEM)
    dma = pltpu.SemaphoreType.DMA
    return pl.pallas_call(
        functools.partial(score_kernel, (dp, layers)),
        out_shape=jax.ShapeDtypeStruct((per * count, n), f32),
        in_specs=[pl.BlockSpec(memory_space=pl.ANY)] + [vmem] * 4,
        out_specs=vmem,
        scratch_shapes=[
            pltpu.VMEM((n, entries), bf16),
            pltpu.VMEM((chips, 2, 2, half, entries), bf16),
            pltpu.VMEM((chips, 2, 2, half, n), f32),
            pltpu.VMEM((chips, 2, 2, half, n), bf16),
            pltpu.VMEM((chips, 2, 2, half, n), bf16),
            pltpu.VMEM((layers // 2, per, 2, half, n), bf16),
            dma,
            dma((chips, chunks)),
            dma((chips, chunks)),
            dma((chips, chunks)),
            dma((chips, chunks)),
            dma((chips, 2, chunks)),
            dma((chips, 2, chunks)),
            dma((chips, 2, 2)),
            dma((layers // 2, per, 2)),
            dma((chips, 2, 2)),
            pltpu.VMEM((4 * D, 4 * D), f32),
            pltpu.VMEM((4 * D, 2 * D), f32),
            pltpu.VMEM((2 * D, 2 * D), f32),
            pltpu.VMEM((entries, count), f32),
            pltpu.VMEM((entries, count), f32),
            pltpu.VMEM((D, 4 * D), f32),
            pltpu.VMEM((D, 4 * D), f32),
            pltpu.VMEM((2 * D, 4 * D), f32),
            pltpu.VMEM((2 * D, 4 * D), bf16),
        ],
        compiler_params=pltpu.CompilerParams(
            collective_id=0, has_side_effects=True, vmem_limit_bytes=VMEM_LIMIT
        ),
        name="scores",
    )(train_rows, grads, bo, bi, s)


def solution(mesh):
    dp, layers = mesh.shape["dp"], mesh.shape["layer"]

    def body(train_grads, query_grads, basis_out, basis_in, scaling):
        return scores(
            train_grads[:, 0, :],
            query_grads[:, 0, :],
            basis_out[0],
            basis_in[0],
            scaling[0],
            dp,
            layers,
        )

    in_specs = (
        P(("groups", "dp"), "layer", None),
        P("dp", "layer", None),
        P("layer", None, None),
        P("layer", None, None),
        P("layer", None, None),
    )
    out_specs = P("layer", ("groups", "dp"))
    return jax.shard_map(body, mesh=mesh, in_specs=in_specs, out_specs=out_specs, check_vma=False)
```
